32 devices in a mesh: seq: 8 (over y, x, core), head: 4 (over z).
Axes of the slice: x: 2, y: 2, z: 4, core: 2. Of those that a mesh axis runs over, the one named last changes fastest.
Arguments:
- hidden: bfloat16 [1024, 3072], P('seq'), may hold values from -6 to 6
- cotangent: bfloat16 [1024, 3072], P('seq'), may hold values from -6 to 6
- mod_scale: float32 [3072], replicated, may hold values from -0.5 to 0.5
- mod_shift: float32 [3072], replicated, may hold values from -3 to 3
- branch_gate: float32 [3072], replicated, may hold values from 0.3 to 1.5
- query_weight: bfloat16 [3072, 1536], P('seq', 'head'), may hold values from -0.108253175 to 0.108253175, as said below
- key_weight: bfloat16 [3072, 1536], P('seq', 'head'), may hold values from -0.108253175 to 0.108253175, as said below
- value_weight: bfloat16 [3072, 1536], P('seq', 'head'), may hold values from -0.109375 to 0.109375
- output_weight: bfloat16 [3072, 1536], P('seq', 'head'), may hold values from -0.15625 to 0.15625
- query_gain: float32 [1536], P('head'), may hold values from 0.7 to 6.3
- key_gain: float32 [1536], P('head'), may hold values from 0.7 to 6.3
Outputs:
- hidden_grad: bfloat16 [1024, 3072], P('seq')
- outproj_grad: float32 [3072, 1536], P('seq', 'head')
The draws below stay inside these ranges and needn't reach their ends.
Inputs may be any that keep to these rules, and one draw needn't show every extreme that they name: `query_weight`: entries of the query projection, of order 3072^-0.5. `key_weight`: entries of the key projection, of order 3072^-0.5.
All inputs are finite; a program needn't handle non-finite values.
Results may differ from the reference program's by a relative error of at most 0.028.
Values may be sent and summed in bfloat16 or wider, within the bound.
A program may use at most 128 MiB of HBM per device.

```python
import math
import jax
import jax.numpy as jnp
from jax import lax

D = 3072
HEADS = 12
HEAD_DIM = 128
SEQ = 1024


def weight_base(key, salt):
    values = jax.random.normal(jax.random.fold_in(key, salt), (D, HEADS * HEAD_DIM), jnp.float32)
    return jnp.clip(values, -6.0, 6.0) / math.sqrt(D)


def draw_query_weight(key, part):
    return weight_base(key, 11).astype(jnp.bfloat16)


def draw_key_weight(key, part):
    return weight_base(key, 12).astype(jnp.bfloat16)


def gain_base(key, salt):
    jitter = jnp.exp(jax.random.uniform(jax.random.fold_in(key, salt), (HEADS, HEAD_DIM), jnp.float32, math.log(0.7), math.log(1.4)))
    return jitter.reshape(-1)


def draw_query_gain(key, part):
    return gain_base(key, 21)


def draw_key_gain(key, part):
    return gain_base(key, 22)


def raised(array, stream_key, source, target, parts, factor):
    owner, partner = [(jnp.arange(array.shape[position]) // (array.shape[position] // parts)).reshape([-1 if axis == position else 1 for axis in range(array.ndim)]) for position in (source, target)]
    chosen = jax.random.permutation(stream_key, parts)[partner]
    strong = (owner == chosen) | (owner == (partner + parts // 2) % parts)
    return jnp.where(strong, factor * array, array)


def block_levels(key, dims, cuts, smallest, largest):
    factor_of, own = 1.0, jax.random.fold_in(key, 6)
    for dim, blocks in cuts:
        steps = jnp.exp(jax.random.uniform(jax.random.fold_in(own, dim), (blocks,), jnp.float32, smallest / len(cuts), largest / len(cuts)))
        factor_of = factor_of * jnp.repeat(steps, dims[dim] // blocks).reshape([-1 if axis == dim else 1 for axis in range(len(dims))])
    return factor_of


def scatter_about(stream_key, shape, spread, most, pieces=(), kind=jnp.bfloat16):
    entries = jax.random.normal(stream_key, shape, jnp.float32) * spread
    if len(pieces) > 0:
        entries = block_levels(stream_key, shape, pieces, -0.22, 0.18) * entries
    return jnp.clip(entries, min=-most, max=most).astype(kind)


def bell_draw_with(own_key, shape, deviation, reach, split, heavy, kind=jnp.bfloat16):
    values = deviation * jax.random.normal(own_key, shape, jnp.float32)
    if split:
        values = values * block_levels(own_key, shape, split, -0.22, 0.18)
    return jnp.clip(raised(values, jax.random.fold_in(own_key, 3), *heavy), -reach, reach).astype(kind)


def setup_inputs(seed: int = 0) -> dict:
    arg_keys = jax.random.split(jax.random.key(seed), 12)
    hidden = scatter_about(arg_keys[0], (SEQ, D), 1.0, 6.0, ((0, 8),))
    cotangent = bell_draw_with(arg_keys[1], (SEQ, D), 1.0, 6.0, ((0, 8),), (0, 1, 8, 2.0))
    mod_scale = jnp.clip(jax.random.uniform(arg_keys[2], (D,), jnp.float32, -0.5, 0.5), -0.5, 0.5)
    mod_shift = scatter_about(arg_keys[3], (D,), 0.5, 3.0, (), jnp.float32)
    branch_gate = jnp.clip(jax.random.uniform(arg_keys[4], (D,), jnp.float32, 0.3, 1.5), 0.3, 1.5)
    query_weight = draw_query_weight(jax.random.fold_in(arg_keys[11], 71), 0)
    key_weight = draw_key_weight(jax.random.fold_in(arg_keys[11], 71), 0)
    value_weight = scatter_about(arg_keys[7], (D, HEADS * HEAD_DIM), D ** -0.5, 0.109375, ((0, 8), (1, 4)))
    output_weight = scatter_about(arg_keys[8], (D, HEADS * HEAD_DIM), (HEADS * HEAD_DIM) ** -0.5, 0.15625, ((0, 8), (1, 4)))
    query_gain = draw_query_gain(jax.random.fold_in(arg_keys[11], 71), 0)
    key_gain = draw_key_gain(jax.random.fold_in(arg_keys[11], 71), 0)
    return dict(hidden=hidden, cotangent=cotangent, mod_scale=mod_scale, mod_shift=mod_shift, branch_gate=branch_gate, query_weight=query_weight, key_weight=key_weight, value_weight=value_weight, output_weight=output_weight, query_gain=query_gain, key_gain=key_gain)


EPSILON = 1e-06

def layer_normed(hidden, mod_scale, mod_shift):
    values = hidden.astype(jnp.float32)
    center = values - lax.optimization_barrier(jnp.mean(values, axis=-1, keepdims=True))
    inverse = lax.rsqrt(lax.optimization_barrier(jnp.mean(center * center, axis=-1, keepdims=True)) + EPSILON)
    unit = center * inverse
    normed = (unit * (1.0 + mod_scale) + mod_shift).astype(jnp.bfloat16)
    return (unit, inverse, normed)

def layer_back(grad, unit, inverse, mod_scale):
    scaled = grad * (1.0 + mod_scale)
    middle = lax.optimization_barrier(jnp.mean(scaled, axis=-1, keepdims=True))
    along = lax.optimization_barrier(jnp.mean(scaled * unit, axis=-1, keepdims=True))
    return inverse * (scaled - middle - unit * along)

def head_norm(raw, gain, factor):
    inverse = lax.rsqrt(lax.optimization_barrier(jnp.mean(raw * raw, axis=-1, keepdims=True)) + EPSILON)
    unit = raw * inverse
    return (unit, inverse, (unit * gain * factor).astype(jnp.bfloat16))

def head_back(grad, unit, inverse, gain, factor):
    scaled = grad * gain * factor
    along = lax.optimization_barrier(jnp.mean(scaled * unit, axis=-1, keepdims=True))
    return (inverse * (scaled - unit * along)).astype(jnp.bfloat16)

def reference(hidden, cotangent, mod_scale, mod_shift, branch_gate, query_weight, key_weight, value_weight, output_weight, query_gain, key_gain):
    factor = jnp.float32(1.0 / math.sqrt(HEAD_DIM))
    rows = hidden.shape[0]
    width = HEADS * HEAD_DIM
    cube = (rows, HEADS, HEAD_DIM)
    unit, inverse, normed = layer_normed(hidden, mod_scale, mod_shift)
    query_raw = jnp.dot(normed, query_weight, preferred_element_type=jnp.float32).reshape(cube)
    key_raw = jnp.dot(normed, key_weight, preferred_element_type=jnp.float32).reshape(cube)
    value_raw = jnp.dot(normed, value_weight, preferred_element_type=jnp.float32).reshape(cube)
    query_unit, query_inverse, query = head_norm(query_raw, query_gain.reshape(HEADS, HEAD_DIM), factor)
    key_unit, key_inverse, keys = head_norm(key_raw, key_gain.reshape(HEADS, HEAD_DIM), jnp.float32(1.0))
    values = value_raw.astype(jnp.bfloat16)
    keys_wide = keys.astype(jnp.float32)
    values_wide = values.astype(jnp.float32)
    block = math.gcd(rows, 512)
    count = rows // block

    def forward_block(query_block):
        scores = jnp.einsum('qhd,khd->hqk', query_block.astype(jnp.float32), keys_wide)
        top = lax.optimization_barrier(jnp.max(scores, axis=-1, keepdims=True))
        expo = jnp.exp(scores - top)
        total = lax.optimization_barrier(jnp.sum(expo, axis=-1, keepdims=True))
        probs = expo.astype(jnp.bfloat16).astype(jnp.float32)
        mixed = jnp.einsum('hqk,khd->hqd', probs, values_wide) / total
        mix = jnp.transpose(mixed, (1, 0, 2)).astype(jnp.bfloat16)
        log_total = jnp.transpose((top + jnp.log(total))[:, :, 0])
        return (mix, log_total)
    mix, log_total = lax.map(forward_block, query.reshape(count, block, HEADS, HEAD_DIM))
    mix = mix.reshape(cube)
    log_total = log_total.reshape(rows, HEADS)
    branch_cot = (cotangent.astype(jnp.float32) * branch_gate).astype(jnp.bfloat16)
    mix_flat = mix.reshape(rows, width)
    outproj_grad = jnp.dot(branch_cot.T, mix_flat, preferred_element_type=jnp.float32)
    mix_grad = jnp.dot(branch_cot, output_weight, preferred_element_type=jnp.float32).astype(jnp.bfloat16).reshape(cube)
    delta = lax.optimization_barrier(jnp.sum(mix_grad.astype(jnp.float32) * mix.astype(jnp.float32), axis=-1))

    def backward_block(carry, inputs):
        key_grad, value_grad = carry
        query_block, grad_block, log_block, delta_block = inputs
        query_wide = query_block.astype(jnp.float32)
        grad_wide = grad_block.astype(jnp.float32)
        scores = jnp.einsum('qhd,khd->hqk', query_wide, keys_wide)
        probs = jnp.exp(scores - jnp.transpose(log_block)[:, :, None])
        prob_grad = jnp.einsum('qhd,khd->hqk', grad_wide, values_wide)
        score_grad = (probs * (prob_grad - jnp.transpose(delta_block)[:, :, None])).astype(jnp.bfloat16).astype(jnp.float32)
        query_grad = jnp.einsum('hqk,khd->qhd', score_grad, keys_wide)
        key_grad = key_grad + jnp.einsum('hqk,qhd->khd', score_grad, query_wide)
        probs_low = probs.astype(jnp.bfloat16).astype(jnp.float32)
        value_grad = value_grad + jnp.einsum('hqk,qhd->khd', probs_low, grad_wide)
        return ((key_grad, value_grad), query_grad)
    zeros = jnp.zeros(cube, jnp.float32)
    inputs = (query.reshape(count, block, HEADS, HEAD_DIM), mix_grad.reshape(count, block, HEADS, HEAD_DIM), log_total.reshape(count, block, HEADS), delta.reshape(count, block, HEADS))
    (key_grad, value_grad), query_grad = lax.scan(backward_block, (zeros, zeros), inputs)
    query_grad = query_grad.reshape(cube)
    query_raw_grad = head_back(query_grad, query_unit, query_inverse, query_gain.reshape(HEADS, HEAD_DIM), factor).reshape(rows, width)
    key_raw_grad = head_back(key_grad, key_unit, key_inverse, key_gain.reshape(HEADS, HEAD_DIM), jnp.float32(1.0)).reshape(rows, width)
    value_raw_grad = value_grad.astype(jnp.bfloat16).reshape(rows, width)
    normed_grad = jnp.dot(query_raw_grad, query_weight.T, preferred_element_type=jnp.float32)
    normed_grad = normed_grad + jnp.dot(key_raw_grad, key_weight.T, preferred_element_type=jnp.float32)
    normed_grad = normed_grad + jnp.dot(value_raw_grad, value_weight.T, preferred_element_type=jnp.float32)
    hidden_grad = layer_back(normed_grad, unit, inverse, mod_scale).astype(jnp.bfloat16)
    return (hidden_grad, outproj_grad)
```

```python
import functools
import math

import jax
import jax.numpy as jnp
from jax import lax
from jax.experimental import pallas as pl
from jax.experimental.pallas import tpu as pltpu
from jax.sharding import PartitionSpec as P

HEAD_DIM = 128
EPSILON = 1e-06
F32 = jnp.float32
BF16 = jnp.bfloat16
K, V, Q, O = range(4)


def dot(a, b):
    return lax.dot_general(a, b, (((1,), (0,)), ((), ())), preferred_element_type=F32)


def dot_t(a, b):
    return lax.dot_general(a, b, (((1,), (1,)), ((), ())), preferred_element_type=F32)


def flipped(me, mask):
    out, bit = me, 0
    while (1 << bit) <= mask:
        if mask >> bit & 1:
            out = out + (1 << bit) * (1 - 2 * (lax.div(me, 1 << bit) % 2))
        bit += 1
    return out


def gather_orders(size):
    bits = [1 << b for b in range(size.bit_length() - 1)]
    return (bits[1:] + bits[:1], bits[1:][::-1] + bits[:1])


def scatter_orders(size):
    bits = [1 << b for b in range(size.bit_length() - 1)]
    return (bits[:1] + bits[1:], bits[:1] + bits[1:][::-1])


class Gather:
    def __init__(self, buf, index, me, size, send, recv):
        self.rows = buf.shape[2]
        self.copies = {}
        self.masks = sorted(range(1, size), key=lambda m: (bin(m).count("1"), m))
        self.orders = gather_orders(size)
        half = self.rows // 2
        for side, order in enumerate(self.orders):
            for mask in self.masks:
                last = [d for d in order if mask & d][-1]
                ref = buf.at[index, flipped(me, mask ^ last), pl.ds(side * half, half)]
                self.copies[side, mask] = pltpu.make_async_remote_copy(
                    src_ref=ref,
                    dst_ref=ref,
                    send_sem=send.at[index, side, mask],
                    recv_sem=recv.at[index, side, mask],
                    device_id={"seq": flipped(me, last)},
                    device_id_type=pl.DeviceIdType.MESH,
                )

    def push(self, side, mask):
        order = self.orders[side]
        start = 0
        for place, d in enumerate(order):
            if mask & d:
                start = place + 1
        for d in order[start:]:
            self.copies[side, mask | d].start()

    def begin(self):
        for side in range(2):
            self.push(side, 0)

    def proceed(self):
        for mask in self.masks:
            for side in range(2):
                self.copies[side, mask].wait_recv()
                self.push(side, mask)

    def finish(self):
        for copy in self.copies.values():
            copy.wait_send()


def kernel(
    seq,
    head,
    hidden_ref,
    cot_ref,
    scale_ref,
    shift_ref,
    gate_ref,
    qw_ref,
    kw_ref,
    vw_ref,
    ow_ref,
    qg_ref,
    kg_ref,
    grad_ref,
    outproj_ref,
    wall,
    act,
    stats,
    normed,
    cot,
    cot_t,
    expo,
    acc,
    rbuf,
    own,
    zs,
    zin,
    zmid,
    ztot,
    wsend,
    wrecv,
    asend,
    arecv,
    ssend,
    srecv,
    rsend,
    rrecv,
    zsend,
    zrecv,
):
    me = lax.axis_index("seq")
    hd = lax.axis_index("head")
    rows, width = hidden_ref.shape
    depth, cols = qw_ref.shape
    heads = cols // HEAD_DIM
    factor = F32(1.0 / math.sqrt(HEAD_DIM))
    mesh_ids = pl.DeviceIdType.MESH

    for index, ref in ((K, kw_ref), (V, vw_ref), (Q, qw_ref), (O, ow_ref)):
        wall[index, me] = ref[...]

    barrier = pltpu.get_barrier_semaphore()
    for step in range(1, seq):
        pl.semaphore_signal(
            barrier, inc=1, device_id={"seq": flipped(me, step)}, device_id_type=mesh_ids
        )
    for step in range(1, head):
        pl.semaphore_signal(
            barrier, inc=1, device_id={"head": (hd + step) % head}, device_id_type=mesh_ids
        )
    pl.semaphore_wait(barrier, seq - 1 + head - 1)

    weights = [Gather(wall, i, me, seq, wsend, wrecv) for i in range(4)]
    acts = [Gather(act, i, me, seq, asend, arecv) for i in range(4)]
    weights[K].begin()
    weights[V].begin()

    values = hidden_ref[...].astype(F32)
    center = values - jnp.mean(values, axis=-1, keepdims=True)
    mean = jnp.mean(values, axis=-1, keepdims=True)
    inverse = lax.rsqrt(jnp.mean(center * center, axis=-1, keepdims=True) + EPSILON)
    normed[...] = (center * inverse * (1.0 + scale_ref[...]) + shift_ref[...]).astype(BF16)
    branch = cot_ref[...].astype(F32) * gate_ref[...]
    cot[...] = branch.astype(BF16)
    cot_t[...] = jnp.transpose(branch).astype(BF16)

    def project(source, index):
        return dot(source[...], wall[index].reshape(width, cols))

    def head_norm(raw, gain_ref, scalar):
        units, inverses, outs = [], [], []
        for h in range(heads):
            part = raw[:, h * HEAD_DIM : (h + 1) * HEAD_DIM]
            inv = lax.rsqrt(jnp.mean(part * part, axis=-1, keepdims=True) + EPSILON)
            unit = part * inv
            gain = gain_ref[:, h * HEAD_DIM : (h + 1) * HEAD_DIM]
            units.append(unit)
            inverses.append(inv)
            outs.append((unit * gain * scalar).astype(BF16))
        return units, inverses, jnp.concatenate(outs, axis=1)

    def head_back(grad, unit, inv, gain, scalar):
        scaled = grad * gain * scalar
        along = jnp.mean(scaled * unit, axis=-1, keepdims=True)
        return (inv * (scaled - unit * along)).astype(BF16)

    weights[K].proceed()
    weights[Q].begin()
    key_unit, key_inverse, keys = head_norm(project(normed, K), kg_ref, F32(1.0))
    act[K, me] = keys
    acts[K].begin()
    weights[V].proceed()
    weights[O].begin()
    act[V, me] = project(normed, V).astype(BF16)
    acts[V].begin()
    weights[Q].proceed()
    query_unit, query_inverse, query = head_norm(project(normed, Q), qg_ref, factor)
    act[Q, me] = query
    acts[Q].begin()
    acts[K].proceed()
    acts[V].proceed()
    weights[O].proceed()
    act[O, me] = project(cot, O).astype(BF16)
    acts[O].begin()
    acts[Q].proceed()

    def lanes(h):
        return slice(h * HEAD_DIM, (h + 1) * HEAD_DIM)

    def whole(index, h):
        return act[index, :, :, lanes(h)].reshape(seq * rows, HEAD_DIM)

    lane = lax.broadcasted_iota(jnp.int32, (rows, rows), 1)
    table = jnp.zeros((rows, rows), F32)
    mixes, scales, deltas = [], [], []
    for h in range(heads):
        scores = dot_t(act[Q, me, :, lanes(h)], whole(K, h))
        top = jnp.max(scores, axis=-1, keepdims=True)
        part = jnp.exp(scores - top)
        total = jnp.sum(part, axis=-1, keepdims=True)
        expo[h] = part
        mix = (dot(part.astype(BF16), whole(V, h)) / total).astype(BF16)
        grad = act[O, me, :, lanes(h)]
        delta = jnp.sum(grad.astype(F32) * mix.astype(F32), axis=-1, keepdims=True)
        table = jnp.where(lane == h, top + jnp.log(total), table)
        table = jnp.where(lane == heads + h, delta, table)
        mixes.append(mix)
        scales.append(1.0 / total)
        deltas.append(delta)
    stats[me] = jnp.transpose(table)[: stats.shape[1]]
    sent = []
    for mask in range(1, seq):
        copy = pltpu.make_async_remote_copy(
            src_ref=stats.at[me],
            dst_ref=stats.at[me],
            send_sem=ssend.at[mask],
            recv_sem=srecv.at[mask],
            device_id={"seq": flipped(me, mask)},
            device_id_type=mesh_ids,
        )
        copy.start()
        sent.append(copy)

    mix_flat = jnp.concatenate(mixes, axis=1)
    for j in range(seq):
        acc[j] = dot(cot_t[j * depth : (j + 1) * depth, :], mix_flat).astype(BF16)

    half = depth // 2
    orders = scatter_orders(seq)
    moves = {}
    for side in range(2):
        for mask in range(1, seq):
            first = [d for d in orders[side] if mask & d][0]
            moves[side, mask] = pltpu.make_async_remote_copy(
                src_ref=acc.at[flipped(me, mask), pl.ds(side * half, half)],
                dst_ref=rbuf.at[mask, pl.ds(side * half, half)],
                send_sem=rsend.at[side, mask],
                recv_sem=rrecv.at[side, mask],
                device_id={"seq": flipped(me, first)},
                device_id_type=mesh_ids,
            )

    def stage(level):
        out = []
        for side in range(2):
            done = sum(orders[side][:level])
            d = orders[side][level]
            out += [(side, m, d) for m in range(1, seq) if m & d and not m & done]
        return out

    def scatter_send(level):
        for side, mask, _ in stage(level):
            moves[side, mask].start()

    def scatter_add(level):
        for side, mask, d in stage(level):
            moves[side, mask].wait_recv()
            span = pl.ds(side * half, half)
            slot = flipped(me, mask ^ d)
            total = acc[slot, span].astype(F32) + rbuf[mask, span].astype(F32)
            if mask == d and level == len(orders[0]) - 1:
                outproj_ref[span, :] = total
            else:
                acc[slot, span] = total.astype(BF16)

    scatter_send(0)
    acts[O].proceed()

    query_raw_grad, key_raw_grad, value_raw_grad = [], [], []
    for h in range(heads):
        prob_grad = dot_t(act[O, me, :, lanes(h)], whole(V, h))
        score_grad = (expo[h] * scales[h] * (prob_grad - deltas[h])).astype(BF16)
        query_grad = dot(score_grad, whole(K, h))
        query_raw_grad.append(
            head_back(query_grad, query_unit[h], query_inverse[h], qg_ref[:, lanes(h)], factor)
        )
    scatter_add(0)
    if len(orders[0]) > 1:
        scatter_send(1)

    for copy in sent:
        copy.wait_recv()
    for h in range(heads):
        log_row = jnp.concatenate([stats[j, h : h + 1, :] for j in range(seq)], axis=1)
        delta_row = jnp.concatenate(
            [stats[j, heads + h : heads + h + 1, :] for j in range(seq)], axis=1
        )
        probs = jnp.exp(dot_t(act[K, me, :, lanes(h)], whole(Q, h)) - log_row)
        prob_grad = dot_t(act[V, me, :, lanes(h)], whole(O, h))
        score_grad = (probs * (prob_grad - delta_row)).astype(BF16)
        key_grad = dot(score_grad, whole(Q, h))
        value_raw_grad.append(dot(probs.astype(BF16), whole(O, h)).astype(BF16))
        key_raw_grad.append(
            head_back(key_grad, key_unit[h], key_inverse[h], kg_ref[:, lanes(h)], F32(1.0))
        )
    query_raw_grad = jnp.concatenate(query_raw_grad, axis=1)
    key_raw_grad = jnp.concatenate(key_raw_grad, axis=1)
    value_raw_grad = jnp.concatenate(value_raw_grad, axis=1)

    chunks, _, chunk = zs.shape
    per = chunk // depth
    mid = head // 2
    left = hd < mid
    inward = jnp.where(left, hd + 1, hd - 1)
    outward = jnp.where(left, hd - 1, hd + 1)
    place = jnp.where(left, hd, head - 1 - hd)
    inner = place == mid - 1

    def zcopy(src, dst, kind, c, target):
        return pltpu.make_async_remote_copy(
            src_ref=src.at[c],
            dst_ref=dst.at[c],
            send_sem=zsend.at[kind, c],
            recv_sem=zrecv.at[kind, c],
            device_id={"head": target},
            device_id_type=mesh_ids,
        )

    to_next = [zcopy(zs, zin, 0, c, inward) for c in range(chunks)]
    to_mid = [zcopy(zs, zmid, 1, c, inward) for c in range(chunks)]
    to_out = [zcopy(ztot, ztot, 2, c, outward) for c in range(chunks)]

    for c in range(chunks):
        def part(index, c=c):
            return wall[index, c * per : (c + 1) * per].reshape(chunk, cols)

        grad = dot_t(query_raw_grad, part(Q))
        grad = grad + dot_t(key_raw_grad, part(K))
        grad = grad + dot_t(value_raw_grad, part(V))
        own[c] = grad

        @pl.when(place == 0)
        def _(c=c):
            zs[c] = own[c].astype(BF16)
            if mid > 1:
                to_next[c].start()
            else:
                to_mid[c].start()

    lag = 2
    for level in range(1, len(orders[0])):
        if level > 1:
            scatter_send(level)
        if level < len(orders[0]) - 1:
            scatter_add(level)

    for c in range(chunks + lag):
        if c < chunks and mid > 1:

            @pl.when(place > 0)
            def _(c=c):
                to_next[c].wait_recv()
                zs[c] = (own[c] + zin[c].astype(F32)).astype(BF16)

                @pl.when(inner)
                def _():
                    to_mid[c].start()

                @pl.when(jnp.logical_not(inner))
                def _():
                    to_next[c].start()

        if c >= lag:
            b = c - lag

            @pl.when(inner)
            def _(b=b):
                to_mid[b].wait_recv()
                ztot[b] = (zs[b].astype(F32) + zmid[b].astype(F32)).astype(BF16)

            @pl.when(jnp.logical_not(inner))
            def _(b=b):
                to_out[b].wait_recv()

            @pl.when(place > 0)
            def _(b=b):
                to_out[b].start()

    scatter_add(len(orders[0]) - 1)

    middle = jnp.zeros((rows, 1), F32)
    along = jnp.zeros((rows, 1), F32)

    def pieces(c):
        span = slice(c * chunk, (c + 1) * chunk)
        unit = (hidden_ref[:, span].astype(F32) - mean) * inverse
        return span, unit, ztot[c].astype(F32) * (1.0 + scale_ref[:, span])

    for c in range(chunks):
        _, unit, scaled = pieces(c)
        middle = middle + jnp.sum(scaled, axis=-1, keepdims=True)
        along = along + jnp.sum(scaled * unit, axis=-1, keepdims=True)
    middle = middle / width
    along = along / width
    for c in range(chunks):
        span, unit, scaled = pieces(c)
        grad_ref[:, span] = (inverse * (scaled - middle - unit * along)).astype(BF16)

    for gather in weights + acts:
        gather.finish()
    for copy in sent:
        copy.wait_send()
    for copy in moves.values():
        copy.wait_send()
    for c in range(chunks):
        if mid > 1:

            @pl.when(jnp.logical_not(inner))
            def _(c=c):
                to_next[c].wait_send()

        @pl.when(inner)
        def _(c=c):
            to_mid[c].wait_send()

        @pl.when(place > 0)
        def _(c=c):
            to_out[c].wait_send()


def body(seq, head, *args):
    hidden, cotangent, mod_scale, mod_shift, branch_gate, qw, kw, vw, ow, qg, kg = args
    rows, width = hidden.shape
    depth, cols = qw.shape
    heads = cols // HEAD_DIM
    chunk = math.lcm(depth, 128)
    chunks = width // chunk
    stat_rows = -(-2 * heads // 8) * 8
    vmem = pl.BlockSpec(memory_space=pltpu.VMEM)
    dma = pltpu.SemaphoreType.DMA
    zshape = (chunks, rows, chunk)
    return tuple(
        pl.pallas_call(
            functools.partial(kernel, seq, head),
            out_shape=(
                jax.ShapeDtypeStruct((rows, width), BF16),
                jax.ShapeDtypeStruct((depth, cols), F32),
            ),
            in_specs=[vmem] * 11,
            out_specs=(vmem, vmem),
            scratch_shapes=[
                pltpu.VMEM((4, seq, depth, cols), BF16),
                pltpu.VMEM((4, seq, rows, cols), BF16),
                pltpu.VMEM((seq, stat_rows, rows), F32),
                pltpu.VMEM((rows, width), BF16),
                pltpu.VMEM((rows, width), BF16),
                pltpu.VMEM((width, rows), BF16),
                pltpu.VMEM((heads, rows, seq * rows), F32),
                pltpu.VMEM((seq, depth, cols), BF16),
                pltpu.VMEM((seq, depth, cols), BF16),
                pltpu.VMEM(zshape, F32),
                pltpu.VMEM(zshape, BF16),
                pltpu.VMEM(zshape, BF16),
                pltpu.VMEM(zshape, BF16),
                pltpu.VMEM(zshape, BF16),
                dma((4, 2, seq)),
                dma((4, 2, seq)),
                dma((4, 2, seq)),
                dma((4, 2, seq)),
                dma((seq,)),
                dma((seq,)),
                dma((2, seq)),
                dma((2, seq)),
                dma((3, chunks)),
                dma((3, chunks)),
            ],
            compiler_params=pltpu.CompilerParams(
                collective_id=0, has_side_effects=True, vmem_limit_bytes=56 * 1024 * 1024
            ),
        )(
            hidden,
            cotangent,
            mod_scale.reshape(1, -1),
            mod_shift.reshape(1, -1),
            branch_gate.reshape(1, -1),
            qw,
            kw,
            vw,
            ow,
            qg.reshape(1, -1),
            kg.reshape(1, -1),
        )
    )


def solution(mesh):
    placed = (
        P("seq", None),
        P("seq", None),
        P(),
        P(),
        P(),
        P("seq", "head"),
        P("seq", "head"),
        P("seq", "head"),
        P("seq", "head"),
        P("head"),
        P("head"),
    )
    return jax.shard_map(
        functools.partial(body, mesh.shape["seq"], mesh.shape["head"]),
        mesh=mesh,
        in_specs=placed,
        out_specs=(P("seq", None), P("seq", "head")),
        check_vma=False,
    )
```

```python
import functools
import math

import jax
import jax.numpy as jnp
from jax import lax
from jax.experimental import pallas as pl
from jax.experimental.pallas import tpu as pltpu
from jax.sharding import PartitionSpec as P

HEAD_DIM = 128
EPSILON = 1e-06
F32 = jnp.float32
BF16 = jnp.bfloat16
K, V, Q, O = range(4)


def dot(a, b):
    return lax.dot_general(a, b, (((1,), (0,)), ((), ())), preferred_element_type=F32)


def dot_t(a, b):
    return lax.dot_general(a, b, (((1,), (1,)), ((), ())), preferred_element_type=F32)


def flipped(me, mask):
    out, bit = me, 0
    while (1 << bit) <= mask:
        if mask >> bit & 1:
            out = out + (1 << bit) * (1 - 2 * (lax.div(me, 1 << bit) % 2))
        bit += 1
    return out


def gather_orders(size):
    bits = [1 << b for b in range(size.bit_length() - 1)]
    return (bits[1:] + bits[:1], bits[1:][::-1] + bits[:1])


def scatter_orders(size):
    bits = [1 << b for b in range(size.bit_length() - 1)]
    return (bits[:1] + bits[1:], bits[:1] + bits[1:][::-1])


class Gather:
    def __init__(self, buf, index, me, size, send, recv):
        self.rows = buf.shape[2]
        self.copies = {}
        self.masks = sorted(range(1, size), key=lambda m: (bin(m).count("1"), m))
        self.orders = gather_orders(size)
        half = self.rows // 2
        for side, order in enumerate(self.orders):
            for mask in self.masks:
                last = [d for d in order if mask & d][-1]
                ref = buf.at[index, flipped(me, mask ^ last), pl.ds(side * half, half)]
                self.copies[side, mask] = pltpu.make_async_remote_copy(
                    src_ref=ref,
                    dst_ref=ref,
                    send_sem=send.at[index, side, mask],
                    recv_sem=recv.at[index, side, mask],
                    device_id={"seq": flipped(me, last)},
                    device_id_type=pl.DeviceIdType.MESH,
                )

    def push(self, side, mask):
        order = self.orders[side]
        start = 0
        for place, d in enumerate(order):
            if mask & d:
                start = place + 1
        for d in order[start:]:
            self.copies[side, mask | d].start()

    def begin(self):
        for side in range(2):
            self.push(side, 0)

    def proceed(self, low=1, high=99):
        for mask in self.masks:
            if not low <= bin(mask).count("1") <= high:
                continue
            for side in range(2):
                self.copies[side, mask].wait_recv()
                self.push(side, mask)

    def finish(self):
        for copy in self.copies.values():
            copy.wait_send()


def kernel(
    seq,
    head,
    hidden_hbm,
    cot_hbm,
    scale_ref,
    shift_ref,
    gate_ref,
    qw_ref,
    kw_ref,
    vw_ref,
    ow_ref,
    qg_ref,
    kg_ref,
    sum_ref,
    rowstat_ref,
    outproj_ref,
    hidden_ref,
    cot_ref,
    wall,
    act,
    stats,
    normed,
    cot,
    cot_t,
    expo,
    acc,
    rbuf,
    own,
    zs,
    zin,
    zmid,
    ztot,
    wsend,
    wrecv,
    asend,
    arecv,
    ssend,
    srecv,
    rsend,
    rrecv,
    zsend,
    zrecv,
    load,
):
    me = lax.axis_index("seq")
    hd = lax.axis_index("head")
    rows, width = hidden_ref.shape
    depth, cols = qw_ref.shape
    heads = cols // HEAD_DIM
    factor = F32(1.0 / math.sqrt(HEAD_DIM))
    mesh_ids = pl.DeviceIdType.MESH

    loads = [
        pltpu.make_async_copy(ref, wall.at[index, me], load.at[index])
        for index, ref in ((K, kw_ref), (V, vw_ref), (Q, qw_ref), (O, ow_ref))
    ]
    loads.insert(2, pltpu.make_async_copy(hidden_hbm, hidden_ref, load.at[4]))
    loads.append(pltpu.make_async_copy(cot_hbm, cot_ref, load.at[5]))
    for copy in loads:
        copy.start()

    barrier = pltpu.get_barrier_semaphore()
    for step in range(1, seq):
        pl.semaphore_signal(
            barrier, inc=1, device_id={"seq": flipped(me, step)}, device_id_type=mesh_ids
        )
    for step in range(1, head):
        pl.semaphore_signal(
            barrier, inc=1, device_id={"head": (hd + step) % head}, device_id_type=mesh_ids
        )
    pl.semaphore_wait(barrier, seq - 1 + head - 1)

    weights = [Gather(wall, i, me, seq, wsend, wrecv) for i in range(4)]
    acts = [Gather(act, i, me, seq, asend, arecv) for i in range(4)]
    loads[0].wait()
    weights[K].begin()
    loads[1].wait()
    weights[V].begin()
    for copy in loads[2:]:
        copy.wait()

    values = hidden_ref[...].astype(F32)
    center = values - jnp.mean(values, axis=-1, keepdims=True)
    mean = jnp.mean(values, axis=-1, keepdims=True)
    inverse = lax.rsqrt(jnp.mean(center * center, axis=-1, keepdims=True) + EPSILON)
    normed[...] = (center * inverse * (1.0 + scale_ref[...]) + shift_ref[...]).astype(BF16)

    def lanes(h):
        return slice(h * HEAD_DIM, (h + 1) * HEAD_DIM)

    def project(source, index):
        return dot(source[...], wall[index].reshape(width, cols))

    def head_norm(raw, gain_ref, scalar):
        units, inverses, outs = [], [], []
        for h in range(heads):
            part = raw[:, h * HEAD_DIM : (h + 1) * HEAD_DIM]
            inv = lax.rsqrt(jnp.mean(part * part, axis=-1, keepdims=True) + EPSILON)
            unit = part * inv
            gain = gain_ref[lanes(h)][None, :]
            units.append(unit)
            inverses.append(inv)
            outs.append((unit * gain * scalar).astype(BF16))
        return units, inverses, jnp.concatenate(outs, axis=1)

    def head_back(grad, unit, inv, gain, scalar):
        scaled = grad * gain * scalar
        along = jnp.mean(scaled * unit, axis=-1, keepdims=True)
        return (inv * (scaled - unit * along)).astype(BF16)

    weights[K].proceed()
    weights[Q].begin()
    key_unit, key_inverse, keys = head_norm(project(normed, K), kg_ref, F32(1.0))
    act[K, me] = keys
    acts[K].begin()
    branch = cot_ref[...].astype(F32) * gate_ref[...]
    cot[...] = branch.astype(BF16)
    cot_t[...] = jnp.transpose(branch).astype(BF16)
    weights[V].proceed()
    weights[O].begin()
    act[V, me] = project(normed, V).astype(BF16)
    acts[V].begin()
    weights[Q].proceed()
    query_unit, query_inverse, query = head_norm(project(normed, Q), qg_ref, factor)
    act[Q, me] = query
    acts[Q].begin()
    weights[O].proceed(1, 1)
    acts[K].proceed(1, 1)
    acts[V].proceed(1, 1)
    weights[O].proceed(2)
    act[O, me] = project(cot, O).astype(BF16)
    acts[O].begin()
    acts[K].proceed(2)
    acts[Q].proceed(1, 1)
    acts[V].proceed(2)

    def whole(index, h):
        return act[index, :, :, lanes(h)].reshape(seq * rows, HEAD_DIM)

    lane = lax.broadcasted_iota(jnp.int32, (rows, rows), 1)
    table = jnp.zeros((rows, rows), F32)
    mixes, scales, deltas = [], [], []
    for h in range(heads):
        scores = dot_t(act[Q, me, :, lanes(h)], whole(K, h))
        top = jnp.max(scores, axis=-1, keepdims=True)
        part = jnp.exp(scores - top)
        total = jnp.sum(part, axis=-1, keepdims=True)
        expo[h] = part
        mix = (dot(part.astype(BF16), whole(V, h)) / total).astype(BF16)
        grad = act[O, me, :, lanes(h)]
        delta = jnp.sum(grad.astype(F32) * mix.astype(F32), axis=-1, keepdims=True)
        table = jnp.where(lane == h, top + jnp.log(total), table)
        table = jnp.where(lane == heads + h, delta, table)
        mixes.append(mix)
        scales.append(1.0 / total)
        deltas.append(delta)
        if h == 0:
            acts[O].proceed(1, 1)
            acts[Q].proceed(2, 2)
        if h == min(1, heads - 1):
            acts[O].proceed(2, 2)
    stats[me] = jnp.transpose(table)[: stats.shape[1]]
    sent = []
    for mask in range(1, seq):
        copy = pltpu.make_async_remote_copy(
            src_ref=stats.at[me],
            dst_ref=stats.at[me],
            send_sem=ssend.at[mask],
            recv_sem=srecv.at[mask],
            device_id={"seq": flipped(me, mask)},
            device_id_type=mesh_ids,
        )
        copy.start()
        sent.append(copy)

    mix_flat = jnp.concatenate(mixes, axis=1)
    half = depth // 2
    orders = scatter_orders(seq)
    moves = {}
    for side in range(2):
        for mask in range(1, seq):
            first = [d for d in orders[side] if mask & d][0]
            moves[side, mask] = pltpu.make_async_remote_copy(
                src_ref=acc.at[flipped(me, mask), pl.ds(side * half, half)],
                dst_ref=rbuf.at[mask, pl.ds(side * half, half)],
                send_sem=rsend.at[side, mask],
                recv_sem=rrecv.at[side, mask],
                device_id={"seq": flipped(me, first)},
                device_id_type=mesh_ids,
            )

    def stage(level):
        out = []
        for side in range(2):
            done = sum(orders[side][:level])
            d = orders[side][level]
            out += [(side, m, d) for m in range(1, seq) if m & d and not m & done]
        return out

    def scatter_send(level):
        for side, mask, _ in stage(level):
            moves[side, mask].start()

    def scatter_add(level):
        for side, mask, d in stage(level):
            moves[side, mask].wait_recv()
            span = pl.ds(side * half, half)
            slot = flipped(me, mask ^ d)
            total = acc[slot, span].astype(F32) + rbuf[mask, span].astype(F32)
            if mask == d and level == len(orders[0]) - 1:
                outproj_ref[span, :] = total
            else:
                acc[slot, span] = total.astype(BF16)

    query_raw_grad, key_raw_grad, value_raw_grad = [], [], []
    for h in range(heads):
        prob_grad = dot_t(act[O, me, :, lanes(h)], whole(V, h))
        score_grad = (expo[h] * scales[h] * (prob_grad - deltas[h])).astype(BF16)
        query_grad = dot(score_grad, whole(K, h))
        query_raw_grad.append(
            head_back(query_grad, query_unit[h], query_inverse[h], qg_ref[lanes(h)][None, :], factor)
        )
    acts[Q].proceed(3)
    acts[O].proceed(3)
    for copy in sent:
        copy.wait_recv()
    for h in range(heads):
        log_row = jnp.concatenate([stats[j, h : h + 1, :] for j in range(seq)], axis=1)
        delta_row = jnp.concatenate(
            [stats[j, heads + h : heads + h + 1, :] for j in range(seq)], axis=1
        )
        probs = jnp.exp(dot_t(act[K, me, :, lanes(h)], whole(Q, h)) - log_row)
        prob_grad = dot_t(act[V, me, :, lanes(h)], whole(O, h))
        score_grad = (probs * (prob_grad - delta_row)).astype(BF16)
        key_grad = dot(score_grad, whole(Q, h))
        value_raw_grad.append(dot(probs.astype(BF16), whole(O, h)).astype(BF16))
        key_raw_grad.append(
            head_back(key_grad, key_unit[h], key_inverse[h], kg_ref[lanes(h)][None, :], F32(1.0))
        )
    query_raw_grad = jnp.concatenate(query_raw_grad, axis=1)
    key_raw_grad = jnp.concatenate(key_raw_grad, axis=1)
    value_raw_grad = jnp.concatenate(value_raw_grad, axis=1)

    messages, split, chunk = zs.shape
    parts = rows // split
    chunks = messages // parts
    per = chunk // depth
    mid = head // 2
    left = hd < mid
    inward = jnp.where(left, hd + 1, hd - 1)
    outward = jnp.where(left, hd - 1, hd + 1)
    place = jnp.where(left, hd, head - 1 - hd)
    inner = place == mid - 1

    def zcopy(src, dst, kind, c, target):
        return pltpu.make_async_remote_copy(
            src_ref=src.at[c],
            dst_ref=dst.at[c],
            send_sem=zsend.at[kind, c],
            recv_sem=zrecv.at[kind, c],
            device_id={"head": target},
            device_id_type=mesh_ids,
        )

    to_next = [zcopy(zs, zin, 0, c, inward) for c in range(messages)]
    to_mid = [zcopy(zs, zmid, 1, c, inward) for c in range(messages)]
    to_out = [zcopy(ztot, ztot, 2, c, outward) for c in range(messages)]

    def own_part(c):
        def part(index):
            return wall[index, c * per : (c + 1) * per].reshape(chunk, cols)

        grad = dot_t(query_raw_grad, part(Q))
        grad = grad + dot_t(key_raw_grad, part(K))
        grad = grad + dot_t(value_raw_grad, part(V))
        for p in range(parts):
            own[c * parts + p] = grad[p * split : (p + 1) * split]

        @pl.when(place == 0)
        def _():
            for b in range(c * parts, (c + 1) * parts):
                zs[b] = own[b].astype(BF16)
                if mid > 1:
                    to_next[b].start()
                else:
                    to_mid[b].start()

    def pass_in(b):
        @pl.when(place > 0)
        def _():
            to_next[b].wait_recv()
            zs[b] = (own[b] + zin[b].astype(F32)).astype(BF16)

            @pl.when(inner)
            def _():
                to_mid[b].start()

            @pl.when(jnp.logical_not(inner))
            def _():
                to_next[b].start()

    middle = [jnp.zeros((split, 1), F32)] * parts
    along = [jnp.zeros((split, 1), F32)] * parts

    def pass_out(b):
        @pl.when(inner)
        def _():
            to_mid[b].wait_recv()
            ztot[b] = (zs[b].astype(F32) + zmid[b].astype(F32)).astype(BF16)

        @pl.when(jnp.logical_not(inner))
        def _():
            to_out[b].wait_recv()

        @pl.when(place > 0)
        def _():
            to_out[b].start()

        c, p = b // parts, b % parts
        span = slice(c * chunk, (c + 1) * chunk)
        tokens = slice(p * split, (p + 1) * split)
        unit = (hidden_ref[tokens, span].astype(F32) - mean[tokens]) * inverse[tokens]
        total = ztot[b]
        sum_ref[tokens, span] = total
        scaled = total.astype(F32) * (1.0 + scale_ref[:, span])
        middle[p] = middle[p] + jnp.sum(scaled, axis=-1, keepdims=True)
        along[p] = along[p] + jnp.sum(scaled * unit, axis=-1, keepdims=True)

    levels = len(orders[0])
    early = max(chunks // 2, 1)
    share = -(-seq // early)
    for c in range(chunks + 3):
        if c < chunks:
            own_part(c)
        for j in range(c * share, min((c + 1) * share, seq)):
            acc[j] = dot(cot_t[j * depth : (j + 1) * depth, :], mix_flat).astype(BF16)
        if c == early - 1:
            scatter_send(0)
        for p in range(parts):
            if 1 <= c <= chunks and mid > 1:
                pass_in((c - 1) * parts + p)
            if c >= 3:
                pass_out((c - 3) * parts + p)
        if c == early + 1:
            scatter_add(0)
            if levels > 1:
                scatter_send(1)
        if c == chunks and levels > 2:
            scatter_add(1)
            scatter_send(2)
    for level in range(min(levels - 1, 2), levels):
        if level > 2:
            scatter_send(level)
        if level > 0:
            scatter_add(level)

    column = lax.broadcasted_iota(jnp.int32, (rows, 128), 1)
    rowstat = jnp.where(column == 0, mean, inverse)
    rowstat = jnp.where(column == 2, jnp.concatenate(middle, axis=0) / width, rowstat)
    rowstat_ref[...] = jnp.where(column == 3, jnp.concatenate(along, axis=0) / width, rowstat)

    for gather in weights + acts:
        gather.finish()
    for copy in sent:
        copy.wait_send()
    for copy in moves.values():
        copy.wait_send()
    for c in range(messages):
        if mid > 1:

            @pl.when(jnp.logical_not(inner))
            def _(c=c):
                to_next[c].wait_send()

        @pl.when(inner)
        def _(c=c):
            to_mid[c].wait_send()

        @pl.when(place > 0)
        def _(c=c):
            to_out[c].wait_send()


def finish(hidden_ref, total_ref, scale_ref, rowstat_ref, outproj_ref, grad_ref, out_ref):
    mean, inverse, middle, along = (rowstat_ref[:, i : i + 1] for i in range(4))
    unit = (hidden_ref[...].astype(F32) - mean) * inverse
    scaled = total_ref[...].astype(F32) * (1.0 + scale_ref[...])
    grad_ref[...] = (inverse * (scaled - middle - unit * along)).astype(BF16)
    out_ref[...] = outproj_ref[...]


def body(seq, head, *args):
    hidden, cotangent, mod_scale, mod_shift, branch_gate, qw, kw, vw, ow, qg, kg = args
    rows, width = hidden.shape
    depth, cols = qw.shape
    heads = cols // HEAD_DIM
    chunk = math.lcm(depth, 128)
    chunks = width // chunk
    stat_rows = -(-2 * heads // 8) * 8
    vmem = pl.BlockSpec(memory_space=pltpu.VMEM)
    dma = pltpu.SemaphoreType.DMA
    parts = 2 if rows % 32 == 0 else 1
    zshape = (chunks * parts, rows // parts, chunk)
    anywhere = pl.BlockSpec(memory_space=pl.ANY)
    total, rowstat, outproj = (
        pl.pallas_call(
            functools.partial(kernel, seq, head),
            out_shape=(
                jax.ShapeDtypeStruct((rows, width), BF16),
                jax.ShapeDtypeStruct((rows, 128), F32),
                jax.ShapeDtypeStruct((depth, cols), F32),
            ),
            in_specs=[anywhere] * 2 + [vmem] * 3 + [anywhere] * 4 + [vmem] * 2,
            out_specs=(vmem, vmem, vmem),
            scratch_shapes=[
                pltpu.VMEM((rows, width), BF16),
                pltpu.VMEM((rows, width), BF16),
                pltpu.VMEM((4, seq, depth, cols), BF16),
                pltpu.VMEM((4, seq, rows, cols), BF16),
                pltpu.VMEM((seq, stat_rows, rows), F32),
                pltpu.VMEM((rows, width), BF16),
                pltpu.VMEM((rows, width), BF16),
                pltpu.VMEM((width, rows), BF16),
                pltpu.VMEM((heads, rows, seq * rows), F32),
                pltpu.VMEM((seq, depth, cols), BF16),
                pltpu.VMEM((seq, depth, cols), BF16),
                pltpu.VMEM(zshape, F32),
                pltpu.VMEM(zshape, BF16),
                pltpu.VMEM(zshape, BF16),
                pltpu.VMEM(zshape, BF16),
                pltpu.VMEM(zshape, BF16),
                dma((4, 2, seq)),
                dma((4, 2, seq)),
                dma((4, 2, seq)),
                dma((4, 2, seq)),
                dma((seq,)),
                dma((seq,)),
                dma((2, seq)),
                dma((2, seq)),
                dma((3, chunks * parts)),
                dma((3, chunks * parts)),
                dma((6,)),
            ],
            compiler_params=pltpu.CompilerParams(
                collective_id=0, has_side_effects=True, vmem_limit_bytes=56 * 1024 * 1024
            ),
        )(
            hidden,
            cotangent,
            mod_scale.reshape(1, -1),
            mod_shift.reshape(1, -1),
            branch_gate.reshape(1, -1),
            qw,
            kw,
            vw,
            ow,
            qg,
            kg,
        )
    )
    steps = 4 if width % 512 == 0 and depth % 32 == 0 else 1
    across = pl.BlockSpec((rows, width // steps), lambda i: (0, i))
    down = pl.BlockSpec((depth // steps, cols), lambda i: (i, 0))
    return tuple(
        pl.pallas_call(
            finish,
            grid=(steps,),
            out_shape=(
                jax.ShapeDtypeStruct((rows, width), BF16),
                jax.ShapeDtypeStruct((depth, cols), F32),
            ),
            in_specs=[
                across,
                across,
                pl.BlockSpec((1, width // steps), lambda i: (0, i)),
                pl.BlockSpec((rows, 128), lambda i: (0, 0)),
                down,
            ],
            out_specs=(across, down),
            compiler_params=pltpu.CompilerParams(vmem_limit_bytes=56 * 1024 * 1024),
        )(hidden, total, mod_scale.reshape(1, -1), rowstat, outproj)
    )


def solution(mesh):
    placed = (
        P("seq", None),
        P("seq", None),
        P(),
        P(),
        P(),
        P("seq", "head"),
        P("seq", "head"),
        P("seq", "head"),
        P("seq", "head"),
        P("head"),
        P("head"),
    )
    return jax.shard_map(
        functools.partial(body, mesh.shape["seq"], mesh.shape["head"]),
        mesh=mesh,
        in_specs=placed,
        out_specs=(P("seq", None), P("seq", "head")),
        check_vma=False,
    )
```

```python
import functools
import math

import jax
import jax.numpy as jnp
from jax import lax
from jax.experimental import pallas as pl
from jax.experimental.pallas import tpu as pltpu
from jax.sharding import PartitionSpec as P

HEAD_DIM = 128
EPSILON = 1e-06
F32 = jnp.float32
BF16 = jnp.bfloat16
K, V, Q, O = range(4)


def dot(a, b):
    return lax.dot_general(a, b, (((1,), (0,)), ((), ())), preferred_element_type=F32)


def dot_t(a, b):
    return lax.dot_general(a, b, (((1,), (1,)), ((), ())), preferred_element_type=F32)


def flipped(me, mask):
    out, bit = me, 0
    while (1 << bit) <= mask:
        if mask >> bit & 1:
            out = out + (1 << bit) * (1 - 2 * (lax.div(me, 1 << bit) % 2))
        bit += 1
    return out


def gather_orders(size):
    bits = [1 << b for b in range(size.bit_length() - 1)]
    return (bits[1:] + bits[:1], bits[1:][::-1] + bits[:1])


def scatter_orders(size):
    bits = [1 << b for b in range(size.bit_length() - 1)]
    return (bits[:1] + bits[1:], bits[:1] + bits[1:][::-1])


class Gather:
    def __init__(self, buf, index, me, size, send, recv):
        self.rows = buf.shape[2]
        self.copies = {}
        self.masks = sorted(range(1, size), key=lambda m: (bin(m).count("1"), m))
        self.orders = gather_orders(size)
        half = self.rows // 2
        for side, order in enumerate(self.orders):
            for mask in self.masks:
                last = [d for d in order if mask & d][-1]
                ref = buf.at[index, flipped(me, mask ^ last), pl.ds(side * half, half)]
                self.copies[side, mask] = pltpu.make_async_remote_copy(
                    src_ref=ref,
                    dst_ref=ref,
                    send_sem=send.at[index, side, mask],
                    recv_sem=recv.at[index, side, mask],
                    device_id={"seq": flipped(me, last)},
                    device_id_type=pl.DeviceIdType.MESH,
                )

    def push(self, side, mask):
        order = self.orders[side]
        start = 0
        for place, d in enumerate(order):
            if mask & d:
                start = place + 1
        for d in order[start:]:
            self.copies[side, mask | d].start()

    def begin(self):
        for side in range(2):
            self.push(side, 0)

    def proceed(self, low=1, high=99):
        for mask in self.masks:
            if not low <= bin(mask).count("1") <= high:
                continue
            for side in range(2):
                self.copies[side, mask].wait_recv()
                self.push(side, mask)

    def finish(self):
        for copy in self.copies.values():
            copy.wait_send()


def kernel(
    seq,
    head,
    hidden_hbm,
    cot_hbm,
    scale_ref,
    shift_ref,
    gate_ref,
    qw_ref,
    kw_ref,
    vw_ref,
    ow_ref,
    qg_ref,
    kg_ref,
    sum_ref,
    rowstat_ref,
    outproj_ref,
    hidden_ref,
    cot_ref,
    wall,
    act,
    stats,
    normed,
    cot,
    cot_t,
    expo,
    acc,
    rbuf,
    own,
    zs,
    zin,
    zmid,
    ztot,
    wsend,
    wrecv,
    asend,
    arecv,
    ssend,
    srecv,
    rsend,
    rrecv,
    zsend,
    zrecv,
    load,
):
    me = lax.axis_index("seq")
    hd = lax.axis_index("head")
    rows, width = hidden_ref.shape
    depth, cols = qw_ref.shape
    heads = cols // HEAD_DIM
    factor = F32(1.0 / math.sqrt(HEAD_DIM))
    mesh_ids = pl.DeviceIdType.MESH

    loads = [
        pltpu.make_async_copy(ref, wall.at[index, me], load.at[index])
        for index, ref in ((K, kw_ref), (V, vw_ref), (Q, qw_ref), (O, ow_ref))
    ]
    loads.insert(2, pltpu.make_async_copy(hidden_hbm, hidden_ref, load.at[4]))
    loads.append(pltpu.make_async_copy(cot_hbm, cot_ref, load.at[5]))
    for copy in loads:
        copy.start()

    barrier = pltpu.get_barrier_semaphore()
    for step in range(1, seq):
        pl.semaphore_signal(
            barrier, inc=1, device_id={"seq": flipped(me, step)}, device_id_type=mesh_ids
        )
    for step in range(1, head):
        pl.semaphore_signal(
            barrier, inc=1, device_id={"head": (hd + step) % head}, device_id_type=mesh_ids
        )
    pl.semaphore_wait(barrier, seq - 1 + head - 1)

    weights = [Gather(wall, i, me, seq, wsend, wrecv) for i in range(4)]
    acts = [Gather(act, i, me, seq, asend, arecv) for i in range(4)]
    loads[0].wait()
    weights[K].begin()
    loads[1].wait()
    weights[V].begin()
    for copy in loads[2:]:
        copy.wait()

    values = hidden_ref[...].astype(F32)
    center = values - jnp.mean(values, axis=-1, keepdims=True)
    mean = jnp.mean(values, axis=-1, keepdims=True)
    inverse = lax.rsqrt(jnp.mean(center * center, axis=-1, keepdims=True) + EPSILON)
    normed[...] = (center * inverse * (1.0 + scale_ref[...]) + shift_ref[...]).astype(BF16)

    def lanes(h):
        return slice(h * HEAD_DIM, (h + 1) * HEAD_DIM)

    def project(source, index):
        return dot(source[...], wall[index].reshape(width, cols))

    def head_norm(raw, gain_ref, scalar):
        units, inverses, outs = [], [], []
        for h in range(heads):
            part = raw[:, h * HEAD_DIM : (h + 1) * HEAD_DIM]
            inv = lax.rsqrt(jnp.mean(part * part, axis=-1, keepdims=True) + EPSILON)
            unit = part * inv
            gain = gain_ref[lanes(h)][None, :]
            units.append(unit)
            inverses.append(inv)
            outs.append((unit * gain * scalar).astype(BF16))
        return units, inverses, jnp.concatenate(outs, axis=1)

    def head_back(grad, unit, inv, gain, scalar):
        scaled = grad * gain * scalar
        along = jnp.mean(scaled * unit, axis=-1, keepdims=True)
        return (inv * (scaled - unit * along)).astype(BF16)

    weights[K].proceed()
    weights[Q].begin()
    key_unit, key_inverse, keys = head_norm(project(normed, K), kg_ref, F32(1.0))
    act[K, me] = keys
    acts[K].begin()
    branch = cot_ref[...].astype(F32) * gate_ref[...]
    cot[...] = branch.astype(BF16)
    cot_t[...] = jnp.transpose(branch).astype(BF16)
    weights[V].proceed()
    act[V, me] = project(normed, V).astype(BF16)
    acts[V].begin()
    weights[Q].proceed(1, 1)
    acts[K].proceed(1, 1)
    weights[O].begin()
    weights[Q].proceed(2)
    query_unit, query_inverse, query = head_norm(project(normed, Q), qg_ref, factor)
    act[Q, me] = query
    acts[Q].begin()
    acts[V].proceed(1, 1)
    acts[K].proceed(2)
    acts[V].proceed(2)

    def whole(index, h):
        return act[index, :, :, lanes(h)].reshape(seq * rows, HEAD_DIM)

    lane = lax.broadcasted_iota(jnp.int32, (rows, rows), 1)
    table = jnp.zeros((rows, rows), F32)
    mixes, scales, logs, deltas = [], [], [], []
    for h in range(heads):
        scores = dot_t(act[Q, me, :, lanes(h)], whole(K, h))
        top = jnp.max(scores, axis=-1, keepdims=True)
        part = jnp.exp(scores - top)
        total = jnp.sum(part, axis=-1, keepdims=True)
        expo[h] = part
        mix = (dot(part.astype(BF16), whole(V, h)) / total).astype(BF16)
        mixes.append(mix)
        scales.append(1.0 / total)
        logs.append(top + jnp.log(total))
        if h == 0:
            weights[O].proceed(1, 1)
            acts[Q].proceed(1, 1)
        if h == min(1, heads - 1):
            weights[O].proceed(2, 2)
    acts[Q].proceed(2, 2)
    weights[O].proceed(3)
    act[O, me] = project(cot, O).astype(BF16)
    acts[O].begin()
    for h in range(heads):
        grad = act[O, me, :, lanes(h)]
        delta = jnp.sum(grad.astype(F32) * mixes[h].astype(F32), axis=-1, keepdims=True)
        table = jnp.where(lane == h, logs[h], table)
        table = jnp.where(lane == heads + h, delta, table)
        deltas.append(delta)
    stats[me] = jnp.transpose(table)[: stats.shape[1]]
    sent = []
    for mask in range(1, seq):
        copy = pltpu.make_async_remote_copy(
            src_ref=stats.at[me],
            dst_ref=stats.at[me],
            send_sem=ssend.at[mask],
            recv_sem=srecv.at[mask],
            device_id={"seq": flipped(me, mask)},
            device_id_type=mesh_ids,
        )
        copy.start()
        sent.append(copy)

    mix_flat = jnp.concatenate(mixes, axis=1)
    half = depth // 2
    orders = scatter_orders(seq)
    moves = {}
    for side in range(2):
        for mask in range(1, seq):
            first = [d for d in orders[side] if mask & d][0]
            moves[side, mask] = pltpu.make_async_remote_copy(
                src_ref=acc.at[flipped(me, mask), pl.ds(side * half, half)],
                dst_ref=rbuf.at[mask, pl.ds(side * half, half)],
                send_sem=rsend.at[side, mask],
                recv_sem=rrecv.at[side, mask],
                device_id={"seq": flipped(me, first)},
                device_id_type=mesh_ids,
            )

    def stage(level):
        out = []
        for side in range(2):
            done = sum(orders[side][:level])
            d = orders[side][level]
            out += [(side, m, d) for m in range(1, seq) if m & d and not m & done]
        return out

    def scatter_send(level):
        for side, mask, _ in stage(level):
            moves[side, mask].start()

    def scatter_add(level):
        for side, mask, d in stage(level):
            moves[side, mask].wait_recv()
            span = pl.ds(side * half, half)
            slot = flipped(me, mask ^ d)
            total = acc[slot, span].astype(F32) + rbuf[mask, span].astype(F32)
            if mask == d and level == len(orders[0]) - 1:
                outproj_ref[span, :] = total
            else:
                acc[slot, span] = total.astype(BF16)

    query_raw_grad, key_raw_grad, value_raw_grad = [], [], []
    for h in range(heads):
        prob_grad = dot_t(act[O, me, :, lanes(h)], whole(V, h))
        score_grad = (expo[h] * scales[h] * (prob_grad - deltas[h])).astype(BF16)
        query_grad = dot(score_grad, whole(K, h))
        query_raw_grad.append(
            head_back(query_grad, query_unit[h], query_inverse[h], qg_ref[lanes(h)][None, :], factor)
        )
        if h == 0:
            acts[O].proceed(1, 1)
            acts[Q].proceed(3)
        if h == min(1, heads - 1):
            acts[O].proceed(2, 2)
    acts[O].proceed(3)
    for copy in sent:
        copy.wait_recv()
    for h in range(heads):
        log_row = jnp.concatenate([stats[j, h : h + 1, :] for j in range(seq)], axis=1)
        delta_row = jnp.concatenate(
            [stats[j, heads + h : heads + h + 1, :] for j in range(seq)], axis=1
        )
        probs = jnp.exp(dot_t(act[K, me, :, lanes(h)], whole(Q, h)) - log_row)
        prob_grad = dot_t(act[V, me, :, lanes(h)], whole(O, h))
        score_grad = (probs * (prob_grad - delta_row)).astype(BF16)
        key_grad = dot(score_grad, whole(Q, h))
        value_raw_grad.append(dot(probs.astype(BF16), whole(O, h)).astype(BF16))
        key_raw_grad.append(
            head_back(key_grad, key_unit[h], key_inverse[h], kg_ref[lanes(h)][None, :], F32(1.0))
        )
    query_raw_grad = jnp.concatenate(query_raw_grad, axis=1)
    key_raw_grad = jnp.concatenate(key_raw_grad, axis=1)
    value_raw_grad = jnp.concatenate(value_raw_grad, axis=1)

    messages, split, chunk = zs.shape
    parts = rows // split
    chunks = messages // parts
    per = chunk // depth
    mid = head // 2
    left = hd < mid
    inward = jnp.where(left, hd + 1, hd - 1)
    outward = jnp.where(left, hd - 1, hd + 1)
    place = jnp.where(left, hd, head - 1 - hd)
    inner = place == mid - 1

    def zcopy(src, dst, kind, c, target):
        return pltpu.make_async_remote_copy(
            src_ref=src.at[c],
            dst_ref=dst.at[c],
            send_sem=zsend.at[kind, c],
            recv_sem=zrecv.at[kind, c],
            device_id={"head": target},
            device_id_type=mesh_ids,
        )

    to_next = [zcopy(zs, zin, 0, c, inward) for c in range(messages)]
    to_mid = [zcopy(zs, zmid, 1, c, inward) for c in range(messages)]
    to_out = [zcopy(ztot, ztot, 2, c, outward) for c in range(messages)]

    def own_part(c):
        def part(index):
            return wall[index, c * per : (c + 1) * per].reshape(chunk, cols)

        grad = dot_t(query_raw_grad, part(Q))
        grad = grad + dot_t(key_raw_grad, part(K))
        grad = grad + dot_t(value_raw_grad, part(V))
        for p in range(parts):
            own[c * parts + p] = grad[p * split : (p + 1) * split]

        @pl.when(place == 0)
        def _():
            for b in range(c * parts, (c + 1) * parts):
                zs[b] = own[b].astype(BF16)
                if mid > 1:
                    to_next[b].start()
                else:
                    to_mid[b].start()

    def pass_in(b):
        @pl.when(place > 0)
        def _():
            to_next[b].wait_recv()
            zs[b] = (own[b] + zin[b].astype(F32)).astype(BF16)

            @pl.when(inner)
            def _():
                to_mid[b].start()

            @pl.when(jnp.logical_not(inner))
            def _():
                to_next[b].start()

    middle = [jnp.zeros((split, 1), F32)] * parts
    along = [jnp.zeros((split, 1), F32)] * parts

    def pass_out(b):
        @pl.when(inner)
        def _():
            to_mid[b].wait_recv()
            ztot[b] = (zs[b].astype(F32) + zmid[b].astype(F32)).astype(BF16)

        @pl.when(jnp.logical_not(inner))
        def _():
            to_out[b].wait_recv()

        @pl.when(place > 0)
        def _():
            to_out[b].start()

        c, p = b // parts, b % parts
        span = slice(c * chunk, (c + 1) * chunk)
        tokens = slice(p * split, (p + 1) * split)
        unit = (hidden_ref[tokens, span].astype(F32) - mean[tokens]) * inverse[tokens]
        total = ztot[b]
        sum_ref[tokens, span] = total
        scaled = total.astype(F32) * (1.0 + scale_ref[:, span])
        middle[p] = middle[p] + jnp.sum(scaled, axis=-1, keepdims=True)
        along[p] = along[p] + jnp.sum(scaled * unit, axis=-1, keepdims=True)

    levels = len(orders[0])
    early = max(chunks // 2, 1)
    share = -(-seq // early)
    for c in range(chunks + 3):
        if c < chunks:
            own_part(c)
        for j in range(c * share, min((c + 1) * share, seq)):
            acc[j] = dot(cot_t[j * depth : (j + 1) * depth, :], mix_flat).astype(BF16)
        if c == early - 1:
            scatter_send(0)
        for p in range(parts):
            if 1 <= c <= chunks and mid > 1:
                pass_in((c - 1) * parts + p)
            if c >= 3:
                pass_out((c - 3) * parts + p)
        if c == early + 1:
            scatter_add(0)
            if levels > 1:
                scatter_send(1)
        if c == chunks and levels > 2:
            scatter_add(1)
            scatter_send(2)
    for level in range(min(levels - 1, 2), levels):
        if level > 2:
            scatter_send(level)
        if level > 0:
            scatter_add(level)

    column = lax.broadcasted_iota(jnp.int32, (rows, 128), 1)
    rowstat = jnp.where(column == 0, mean, inverse)
    rowstat = jnp.where(column == 2, jnp.concatenate(middle, axis=0) / width, rowstat)
    rowstat_ref[...] = jnp.where(column == 3, jnp.concatenate(along, axis=0) / width, rowstat)

    for gather in weights + acts:
        gather.finish()
    for copy in sent:
        copy.wait_send()
    for copy in moves.values():
        copy.wait_send()
    for c in range(messages):
        if mid > 1:

            @pl.when(jnp.logical_not(inner))
            def _(c=c):
                to_next[c].wait_send()

        @pl.when(inner)
        def _(c=c):
            to_mid[c].wait_send()

        @pl.when(place > 0)
        def _(c=c):
            to_out[c].wait_send()


def finish(hidden_ref, total_ref, scale_ref, rowstat_ref, outproj_ref, grad_ref, out_ref):
    mean, inverse, middle, along = (rowstat_ref[:, i : i + 1] for i in range(4))
    unit = (hidden_ref[...].astype(F32) - mean) * inverse
    scaled = total_ref[...].astype(F32) * (1.0 + scale_ref[...])
    grad_ref[...] = (inverse * (scaled - middle - unit * along)).astype(BF16)
    out_ref[...] = outproj_ref[...]


def body(seq, head, *args):
    hidden, cotangent, mod_scale, mod_shift, branch_gate, qw, kw, vw, ow, qg, kg = args
    rows, width = hidden.shape
    depth, cols = qw.shape
    heads = cols // HEAD_DIM
    chunk = math.lcm(depth, 128)
    chunks = width // chunk
    stat_rows = -(-2 * heads // 8) * 8
    vmem = pl.BlockSpec(memory_space=pltpu.VMEM)
    dma = pltpu.SemaphoreType.DMA
    parts = 2 if rows % 32 == 0 else 1
    zshape = (chunks * parts, rows // parts, chunk)
    anywhere = pl.BlockSpec(memory_space=pl.ANY)
    total, rowstat, outproj = (
        pl.pallas_call(
            functools.partial(kernel, seq, head),
            out_shape=(
                jax.ShapeDtypeStruct((rows, width), BF16),
                jax.ShapeDtypeStruct((rows, 128), F32),
                jax.ShapeDtypeStruct((depth, cols), F32),
            ),
            in_specs=[anywhere] * 2 + [vmem] * 3 + [anywhere] * 4 + [vmem] * 2,
            out_specs=(vmem, vmem, vmem),
            scratch_shapes=[
                pltpu.VMEM((rows, width), BF16),
                pltpu.VMEM((rows, width), BF16),
                pltpu.VMEM((4, seq, depth, cols), BF16),
                pltpu.VMEM((4, seq, rows, cols), BF16),
                pltpu.VMEM((seq, stat_rows, rows), F32),
                pltpu.VMEM((rows, width), BF16),
                pltpu.VMEM((rows, width), BF16),
                pltpu.VMEM((width, rows), BF16),
                pltpu.VMEM((heads, rows, seq * rows), F32),
                pltpu.VMEM((seq, depth, cols), BF16),
                pltpu.VMEM((seq, depth, cols), BF16),
                pltpu.VMEM(zshape, F32),
                pltpu.VMEM(zshape, BF16),
                pltpu.VMEM(zshape, BF16),
                pltpu.VMEM(zshape, BF16),
                pltpu.VMEM(zshape, BF16),
                dma((4, 2, seq)),
                dma((4, 2, seq)),
                dma((4, 2, seq)),
                dma((4, 2, seq)),
                dma((seq,)),
                dma((seq,)),
                dma((2, seq)),
                dma((2, seq)),
                dma((3, chunks * parts)),
                dma((3, chunks * parts)),
                dma((6,)),
            ],
            compiler_params=pltpu.CompilerParams(
                collective_id=0, has_side_effects=True, vmem_limit_bytes=56 * 1024 * 1024
            ),
        )(
            hidden,
            cotangent,
            mod_scale.reshape(1, -1),
            mod_shift.reshape(1, -1),
            branch_gate.reshape(1, -1),
            qw,
            kw,
            vw,
            ow,
            qg,
            kg,
        )
    )
    steps = 2 if width % 256 == 0 and depth % 16 == 0 else 1
    across = pl.BlockSpec((rows, width // steps), lambda i: (0, i))
    down = pl.BlockSpec((depth // steps, cols), lambda i: (i, 0))
    return tuple(
        pl.pallas_call(
            finish,
            grid=(steps,),
            out_shape=(
                jax.ShapeDtypeStruct((rows, width), BF16),
                jax.ShapeDtypeStruct((depth, cols), F32),
            ),
            in_specs=[
                across,
                across,
                pl.BlockSpec((1, width // steps), lambda i: (0, i)),
                pl.BlockSpec((rows, 128), lambda i: (0, 0)),
                down,
            ],
            out_specs=(across, down),
            compiler_params=pltpu.CompilerParams(vmem_limit_bytes=56 * 1024 * 1024),
        )(hidden, total, mod_scale.reshape(1, -1), rowstat, outproj)
    )


def solution(mesh):
    placed = (
        P("seq", None),
        P("seq", None),
        P(),
        P(),
        P(),
        P("seq", "head"),
        P("seq", "head"),
        P("seq", "head"),
        P("seq", "head"),
        P("head"),
        P("head"),
    )
    return jax.shard_map(
        functools.partial(body, mesh.shape["seq"], mesh.shape["head"]),
        mesh=mesh,
        in_specs=placed,
        out_specs=(P("seq", None), P("seq", "head")),
        check_vma=False,
    )
```

```python
import functools
import math

import jax
import jax.numpy as jnp
from jax import lax
from jax.experimental import pallas as pl
from jax.experimental.pallas import tpu as pltpu
from jax.sharding import PartitionSpec as P

HEAD_DIM = 128
EPSILON = 1e-06
F32 = jnp.float32
BF16 = jnp.bfloat16
K, V, Q, O = range(4)


def dot(a, b):
    return lax.dot_general(a, b, (((1,), (0,)), ((), ())), preferred_element_type=F32)


def dot_t(a, b):
    return lax.dot_general(a, b, (((1,), (1,)), ((), ())), preferred_element_type=F32)


def flipped(me, mask):
    out, bit = me, 0
    while (1 << bit) <= mask:
        if mask >> bit & 1:
            out = out + (1 << bit) * (1 - 2 * (lax.div(me, 1 << bit) % 2))
        bit += 1
    return out


def gather_orders(size):
    bits = [1 << b for b in range(size.bit_length() - 1)]
    return (bits[1:] + bits[:1], bits[1:][::-1] + bits[:1])


def scatter_orders(size):
    bits = [1 << b for b in range(size.bit_length() - 1)]
    return (bits[:1] + bits[1:], bits[:1] + bits[1:][::-1])


class Gather:
    def __init__(self, buf, index, me, size, send, recv):
        self.rows = buf.shape[2]
        self.copies = {}
        self.masks = sorted(range(1, size), key=lambda m: (bin(m).count("1"), m))
        self.orders = gather_orders(size)
        half = self.rows // 2
        for side, order in enumerate(self.orders):
            for mask in self.masks:
                last = [d for d in order if mask & d][-1]
                ref = buf.at[index, flipped(me, mask ^ last), pl.ds(side * half, half)]
                self.copies[side, mask] = pltpu.make_async_remote_copy(
                    src_ref=ref,
                    dst_ref=ref,
                    send_sem=send.at[index, side, mask],
                    recv_sem=recv.at[index, side, mask],
                    device_id={"seq": flipped(me, last)},
                    device_id_type=pl.DeviceIdType.MESH,
                )

    def push(self, side, mask):
        order = self.orders[side]
        start = 0
        for place, d in enumerate(order):
            if mask & d:
                start = place + 1
        for d in order[start:]:
            self.copies[side, mask | d].start()

    def begin(self):
        for side in range(2):
            self.push(side, 0)

    def proceed(self, low=1, high=99):
        for mask in self.masks:
            if not low <= bin(mask).count("1") <= high:
                continue
            for side in range(2):
                self.copies[side, mask].wait_recv()
                self.push(side, mask)

    def finish(self):
        for copy in self.copies.values():
            copy.wait_send()


def kernel(
    seq,
    head,
    hidden_hbm,
    cot_hbm,
    scale_ref,
    shift_ref,
    gate_ref,
    qw_ref,
    kw_ref,
    vw_ref,
    ow_ref,
    qg_ref,
    kg_ref,
    sum_ref,
    rowstat_ref,
    outproj_ref,
    hidden_ref,
    cot_ref,
    wall,
    act,
    stats,
    normed,
    cot,
    cot_t,
    expo,
    acc,
    rbuf,
    own,
    zs,
    zin,
    zmid,
    ztot,
    wsend,
    wrecv,
    asend,
    arecv,
    ssend,
    srecv,
    rsend,
    rrecv,
    zsend,
    zrecv,
    load,
):
    me = lax.axis_index("seq")
    hd = lax.axis_index("head")
    rows, width = hidden_ref.shape
    depth, cols = qw_ref.shape
    heads = cols // HEAD_DIM
    factor = F32(1.0 / math.sqrt(HEAD_DIM))
    mesh_ids = pl.DeviceIdType.MESH

    loads = [
        pltpu.make_async_copy(ref, wall.at[index, me], load.at[index])
        for index, ref in ((K, kw_ref), (V, vw_ref), (Q, qw_ref), (O, ow_ref))
    ]
    loads.insert(2, pltpu.make_async_copy(hidden_hbm, hidden_ref, load.at[4]))
    loads.append(pltpu.make_async_copy(cot_hbm, cot_ref, load.at[5]))
    for copy in loads:
        copy.start()

    barrier = pltpu.get_barrier_semaphore()
    for step in range(1, seq):
        pl.semaphore_signal(
            barrier, inc=1, device_id={"seq": flipped(me, step)}, device_id_type=mesh_ids
        )
    for step in range(1, head):
        pl.semaphore_signal(
            barrier, inc=1, device_id={"head": (hd + step) % head}, device_id_type=mesh_ids
        )
    pl.semaphore_wait(barrier, seq - 1 + head - 1)

    weights = [Gather(wall, i, me, seq, wsend, wrecv) for i in range(4)]
    acts = [Gather(act, i, me, seq, asend, arecv) for i in range(4)]
    loads[0].wait()
    weights[K].begin()
    loads[1].wait()
    weights[V].begin()
    for copy in loads[2:]:
        copy.wait()

    values = hidden_ref[...].astype(F32)
    center = values - jnp.mean(values, axis=-1, keepdims=True)
    mean = jnp.mean(values, axis=-1, keepdims=True)
    inverse = lax.rsqrt(jnp.mean(center * center, axis=-1, keepdims=True) + EPSILON)
    normed[...] = (center * inverse * (1.0 + scale_ref[...]) + shift_ref[...]).astype(BF16)

    def lanes(h):
        return slice(h * HEAD_DIM, (h + 1) * HEAD_DIM)

    def project(source, index):
        return dot(source[...], wall[index].reshape(width, cols))

    def head_norm(raw, gain_ref, scalar):
        units, inverses, outs = [], [], []
        for h in range(heads):
            part = raw[:, h * HEAD_DIM : (h + 1) * HEAD_DIM]
            inv = lax.rsqrt(jnp.mean(part * part, axis=-1, keepdims=True) + EPSILON)
            unit = part * inv
            gain = gain_ref[lanes(h)][None, :]
            units.append(unit)
            inverses.append(inv)
            outs.append((unit * gain * scalar).astype(BF16))
        return units, inverses, jnp.concatenate(outs, axis=1)

    def head_back(grad, unit, inv, gain, scalar):
        scaled = grad * gain * scalar
        along = jnp.mean(scaled * unit, axis=-1, keepdims=True)
        return (inv * (scaled - unit * along)).astype(BF16)

    weights[K].proceed()
    weights[Q].begin()
    key_unit, key_inverse, keys = head_norm(project(normed, K), kg_ref, F32(1.0))
    act[K, me] = keys
    acts[K].begin()
    branch = cot_ref[...].astype(F32) * gate_ref[...]
    cot[...] = branch.astype(BF16)
    cot_t[...] = jnp.transpose(branch).astype(BF16)
    weights[V].proceed()
    act[V, me] = project(normed, V).astype(BF16)
    acts[V].begin()
    weights[Q].proceed(1, 1)
    acts[K].proceed(1, 1)
    weights[O].begin()
    weights[Q].proceed(2)
    query_unit, query_inverse, query = head_norm(project(normed, Q), qg_ref, factor)
    act[Q, me] = query
    acts[Q].begin()
    acts[V].proceed(1, 1)
    acts[K].proceed(2)
    acts[V].proceed(2)

    def whole(index, h):
        return act[index, :, :, lanes(h)].reshape(seq * rows, HEAD_DIM)

    lane = lax.broadcasted_iota(jnp.int32, (rows, rows), 1)
    table = jnp.zeros((rows, rows), F32)
    mixes, scales, logs, deltas = [], [], [], []
    for h in range(heads):
        scores = dot_t(act[Q, me, :, lanes(h)], whole(K, h))
        top = jnp.max(scores, axis=-1, keepdims=True)
        part = jnp.exp(scores - top)
        total = jnp.sum(part, axis=-1, keepdims=True)
        expo[h] = part
        mix = (dot(part.astype(BF16), whole(V, h)) / total).astype(BF16)
        mixes.append(mix)
        scales.append(1.0 / total)
        logs.append(top + jnp.log(total))
        if h == 0:
            weights[O].proceed(1, 1)
            acts[Q].proceed(1, 1)
        if h == min(1, heads - 1):
            weights[O].proceed(2, 2)
    mix_flat = jnp.concatenate(mixes, axis=1)
    half = depth // 2
    orders = scatter_orders(seq)
    moves = {}
    for side in range(2):
        for mask in range(1, seq):
            first = [d for d in orders[side] if mask & d][0]
            moves[side, mask] = pltpu.make_async_remote_copy(
                src_ref=acc.at[flipped(me, mask), pl.ds(side * half, half)],
                dst_ref=rbuf.at[mask, pl.ds(side * half, half)],
                send_sem=rsend.at[side, mask],
                recv_sem=rrecv.at[side, mask],
                device_id={"seq": flipped(me, first)},
                device_id_type=mesh_ids,
            )

    def stage(level):
        out = []
        for side in range(2):
            done = sum(orders[side][:level])
            d = orders[side][level]
            out += [(side, m, d) for m in range(1, seq) if m & d and not m & done]
        return out

    def scatter_send(level):
        for side, mask, _ in stage(level):
            moves[side, mask].start()

    def scatter_add(level):
        for side, mask, d in stage(level):
            moves[side, mask].wait_recv()
            span = pl.ds(side * half, half)
            slot = flipped(me, mask ^ d)
            total = acc[slot, span].astype(F32) + rbuf[mask, span].astype(F32)
            if mask == d and level == len(orders[0]) - 1:
                outproj_ref[span, :] = total
            else:
                acc[slot, span] = total.astype(BF16)

    levels = len(orders[0])
    for j in range(seq):
        acc[j] = dot(cot_t[j * depth : (j + 1) * depth, :], mix_flat).astype(BF16)
    scatter_send(0)

    acts[Q].proceed(2, 2)
    weights[O].proceed(3)
    act[O, me] = project(cot, O).astype(BF16)
    acts[O].begin()
    for h in range(heads):
        grad = act[O, me, :, lanes(h)]
        delta = jnp.sum(grad.astype(F32) * mixes[h].astype(F32), axis=-1, keepdims=True)
        table = jnp.where(lane == h, logs[h], table)
        table = jnp.where(lane == heads + h, delta, table)
        deltas.append(delta)
    stats[me] = jnp.transpose(table)[: stats.shape[1]]
    sent = []
    for mask in range(1, seq):
        copy = pltpu.make_async_remote_copy(
            src_ref=stats.at[me],
            dst_ref=stats.at[me],
            send_sem=ssend.at[mask],
            recv_sem=srecv.at[mask],
            device_id={"seq": flipped(me, mask)},
            device_id_type=mesh_ids,
        )
        copy.start()
        sent.append(copy)

    query_raw_grad, key_raw_grad, value_raw_grad = [], [], []
    for h in range(heads):
        prob_grad = dot_t(act[O, me, :, lanes(h)], whole(V, h))
        score_grad = (expo[h] * scales[h] * (prob_grad - deltas[h])).astype(BF16)
        query_grad = dot(score_grad, whole(K, h))
        query_raw_grad.append(
            head_back(query_grad, query_unit[h], query_inverse[h], qg_ref[lanes(h)][None, :], factor)
        )
        if h == 0:
            acts[O].proceed(1, 1)
            acts[Q].proceed(3)
        if h == min(1, heads - 1):
            acts[O].proceed(2, 2)
    acts[O].proceed(3)
    if levels > 1:
        scatter_add(0)
        scatter_send(1)
    for copy in sent:
        copy.wait_recv()
    for h in range(heads):
        log_row = jnp.concatenate([stats[j, h : h + 1, :] for j in range(seq)], axis=1)
        delta_row = jnp.concatenate(
            [stats[j, heads + h : heads + h + 1, :] for j in range(seq)], axis=1
        )
        probs = jnp.exp(dot_t(act[K, me, :, lanes(h)], whole(Q, h)) - log_row)
        prob_grad = dot_t(act[V, me, :, lanes(h)], whole(O, h))
        score_grad = (probs * (prob_grad - delta_row)).astype(BF16)
        key_grad = dot(score_grad, whole(Q, h))
        value_raw_grad.append(dot(probs.astype(BF16), whole(O, h)).astype(BF16))
        key_raw_grad.append(
            head_back(key_grad, key_unit[h], key_inverse[h], kg_ref[lanes(h)][None, :], F32(1.0))
        )
    query_raw_grad = jnp.concatenate(query_raw_grad, axis=1)
    key_raw_grad = jnp.concatenate(key_raw_grad, axis=1)
    value_raw_grad = jnp.concatenate(value_raw_grad, axis=1)

    messages, split, chunk = zs.shape
    parts = rows // split
    chunks = messages // parts
    per = chunk // depth
    mid = head // 2
    left = hd < mid
    inward = jnp.where(left, hd + 1, hd - 1)
    outward = jnp.where(left, hd - 1, hd + 1)
    place = jnp.where(left, hd, head - 1 - hd)
    inner = place == mid - 1

    def zcopy(src, dst, kind, c, target):
        return pltpu.make_async_remote_copy(
            src_ref=src.at[c],
            dst_ref=dst.at[c],
            send_sem=zsend.at[kind, c],
            recv_sem=zrecv.at[kind, c],
            device_id={"head": target},
            device_id_type=mesh_ids,
        )

    to_next = [zcopy(zs, zin, 0, c, inward) for c in range(messages)]
    to_mid = [zcopy(zs, zmid, 1, c, inward) for c in range(messages)]
    to_out = [zcopy(ztot, ztot, 2, c, outward) for c in range(messages)]

    def own_part(c):
        def part(index):
            return wall[index, c * per : (c + 1) * per].reshape(chunk, cols)

        grad = dot_t(query_raw_grad, part(Q))
        grad = grad + dot_t(key_raw_grad, part(K))
        grad = grad + dot_t(value_raw_grad, part(V))
        for p in range(parts):
            own[c * parts + p] = grad[p * split : (p + 1) * split]

        @pl.when(place == 0)
        def _():
            for b in range(c * parts, (c + 1) * parts):
                zs[b] = own[b].astype(BF16)
                if mid > 1:
                    to_next[b].start()
                else:
                    to_mid[b].start()

    def pass_in(b):
        @pl.when(place > 0)
        def _():
            to_next[b].wait_recv()
            zs[b] = (own[b] + zin[b].astype(F32)).astype(BF16)

            @pl.when(inner)
            def _():
                to_mid[b].start()

            @pl.when(jnp.logical_not(inner))
            def _():
                to_next[b].start()

    middle = [jnp.zeros((split, 1), F32)] * parts
    along = [jnp.zeros((split, 1), F32)] * parts

    def pass_out(b):
        @pl.when(inner)
        def _():
            to_mid[b].wait_recv()
            ztot[b] = (zs[b].astype(F32) + zmid[b].astype(F32)).astype(BF16)

        @pl.when(jnp.logical_not(inner))
        def _():
            to_out[b].wait_recv()

        @pl.when(place > 0)
        def _():
            to_out[b].start()

        c, p = b // parts, b % parts
        span = slice(c * chunk, (c + 1) * chunk)
        tokens = slice(p * split, (p + 1) * split)
        unit = (hidden_ref[tokens, span].astype(F32) - mean[tokens]) * inverse[tokens]
        total = ztot[b]
        sum_ref[tokens, span] = total
        scaled = total.astype(F32) * (1.0 + scale_ref[:, span])
        middle[p] = middle[p] + jnp.sum(scaled, axis=-1, keepdims=True)
        along[p] = along[p] + jnp.sum(scaled * unit, axis=-1, keepdims=True)

    for c in range(chunks + 3):
        if c < chunks:
            own_part(c)
        for p in range(parts):
            if 1 <= c <= chunks and mid > 1:
                pass_in((c - 1) * parts + p)
            if c >= 3:
                pass_out((c - 3) * parts + p)
        if c == min(2, chunks) and levels > 2:
            scatter_add(1)
            scatter_send(2)
    for level in range(min(levels - 1, 2), levels):
        if level > 2:
            scatter_send(level)
        scatter_add(level)

    column = lax.broadcasted_iota(jnp.int32, (rows, 128), 1)
    rowstat = jnp.where(column == 0, mean, inverse)
    rowstat = jnp.where(column == 2, jnp.concatenate(middle, axis=0) / width, rowstat)
    rowstat_ref[...] = jnp.where(column == 3, jnp.concatenate(along, axis=0) / width, rowstat)

    for gather in weights + acts:
        gather.finish()
    for copy in sent:
        copy.wait_send()
    for copy in moves.values():
        copy.wait_send()
    for c in range(messages):
        if mid > 1:

            @pl.when(jnp.logical_not(inner))
            def _(c=c):
                to_next[c].wait_send()

        @pl.when(inner)
        def _(c=c):
            to_mid[c].wait_send()

        @pl.when(place > 0)
        def _(c=c):
            to_out[c].wait_send()


def finish(hidden_ref, total_ref, scale_ref, rowstat_ref, outproj_ref, grad_ref, out_ref):
    mean, inverse, middle, along = (rowstat_ref[:, i : i + 1] for i in range(4))
    unit = (hidden_ref[...].astype(F32) - mean) * inverse
    scaled = total_ref[...].astype(F32) * (1.0 + scale_ref[...])
    grad_ref[...] = (inverse * (scaled - middle - unit * along)).astype(BF16)
    out_ref[...] = outproj_ref[...]


def body(seq, head, *args):
    hidden, cotangent, mod_scale, mod_shift, branch_gate, qw, kw, vw, ow, qg, kg = args
    rows, width = hidden.shape
    depth, cols = qw.shape
    heads = cols // HEAD_DIM
    chunk = math.lcm(depth, 128)
    chunks = width // chunk
    stat_rows = -(-2 * heads // 8) * 8
    vmem = pl.BlockSpec(memory_space=pltpu.VMEM)
    dma = pltpu.SemaphoreType.DMA
    parts = 2 if rows % 32 == 0 else 1
    zshape = (chunks * parts, rows // parts, chunk)
    anywhere = pl.BlockSpec(memory_space=pl.ANY)
    total, rowstat, outproj = (
        pl.pallas_call(
            functools.partial(kernel, seq, head),
            out_shape=(
                jax.ShapeDtypeStruct((rows, width), BF16),
                jax.ShapeDtypeStruct((rows, 128), F32),
                jax.ShapeDtypeStruct((depth, cols), F32),
            ),
            in_specs=[anywhere] * 2 + [vmem] * 3 + [anywhere] * 4 + [vmem] * 2,
            out_specs=(vmem, vmem, vmem),
            scratch_shapes=[
                pltpu.VMEM((rows, width), BF16),
                pltpu.VMEM((rows, width), BF16),
                pltpu.VMEM((4, seq, depth, cols), BF16),
                pltpu.VMEM((4, seq, rows, cols), BF16),
                pltpu.VMEM((seq, stat_rows, rows), F32),
                pltpu.VMEM((rows, width), BF16),
                pltpu.VMEM((rows, width), BF16),
                pltpu.VMEM((width, rows), BF16),
                pltpu.VMEM((heads, rows, seq * rows), F32),
                pltpu.VMEM((seq, depth, cols), BF16),
                pltpu.VMEM((seq, depth, cols), BF16),
                pltpu.VMEM(zshape, F32),
                pltpu.VMEM(zshape, BF16),
                pltpu.VMEM(zshape, BF16),
                pltpu.VMEM(zshape, BF16),
                pltpu.VMEM(zshape, BF16),
                dma((4, 2, seq)),
                dma((4, 2, seq)),
                dma((4, 2, seq)),
                dma((4, 2, seq)),
                dma((seq,)),
                dma((seq,)),
                dma((2, seq)),
                dma((2, seq)),
                dma((3, chunks * parts)),
                dma((3, chunks * parts)),
                dma((6,)),
            ],
            compiler_params=pltpu.CompilerParams(
                collective_id=0, has_side_effects=True, vmem_limit_bytes=56 * 1024 * 1024
            ),
        )(
            hidden,
            cotangent,
            mod_scale.reshape(1, -1),
            mod_shift.reshape(1, -1),
            branch_gate.reshape(1, -1),
            qw,
            kw,
            vw,
            ow,
            qg,
            kg,
        )
    )
    steps = 2 if width % 256 == 0 and depth % 16 == 0 else 1
    across = pl.BlockSpec((rows, width // steps), lambda i: (0, i))
    down = pl.BlockSpec((depth // steps, cols), lambda i: (i, 0))
    return tuple(
        pl.pallas_call(
            finish,
            grid=(steps,),
            out_shape=(
                jax.ShapeDtypeStruct((rows, width), BF16),
                jax.ShapeDtypeStruct((depth, cols), F32),
            ),
            in_specs=[
                across,
                across,
                pl.BlockSpec((1, width // steps), lambda i: (0, i)),
                pl.BlockSpec((rows, 128), lambda i: (0, 0)),
                down,
            ],
            out_specs=(across, down),
            compiler_params=pltpu.CompilerParams(vmem_limit_bytes=56 * 1024 * 1024),
        )(hidden, total, mod_scale.reshape(1, -1), rowstat, outproj)
    )


def solution(mesh):
    placed = (
        P("seq", None),
        P("seq", None),
        P(),
        P(),
        P(),
        P("seq", "head"),
        P("seq", "head"),
        P("seq", "head"),
        P("seq", "head"),
        P("head"),
        P("head"),
    )
    return jax.shard_map(
        functools.partial(body, mesh.shape["seq"], mesh.shape["head"]),
        mesh=mesh,
        in_specs=placed,
        out_specs=(P("seq", None), P("seq", "head")),
        check_vma=False,
    )
```
